256 devices in a mesh: dp: 2 (over y_hi), hid: 16 (over z, y_lo), ffn: 8 (over x, core).
Axes of the slice: x: 4, y: 4 (y_hi: 2, y_lo: 2; y = y_hi * 2 + y_lo), z: 8, core: 2. Of those that a mesh axis runs over, the one named last changes fastest.
Arguments:
- tokens: bfloat16 [1024, 6144], P('dp', 'hid'), may hold values from -6 to 6
- gate_weight: bfloat16 [6144, 14336], P('hid', 'ffn'), may hold values from -0.078125 to 0.078125
- up_weight: bfloat16 [6144, 14336], P('hid', 'ffn'), may hold values from -0.078125 to 0.078125
- down_weight: bfloat16 [14336, 6144], P('ffn', 'hid'), may hold values from -0.046875 to 0.046875
- gate_tangent: bfloat16 [6144, 14336], P('hid', 'ffn'), may hold values from -0.078125 to 0.078125
- up_tangent: bfloat16 [6144, 14336], P('hid', 'ffn'), may hold values from -0.078125 to 0.078125
- down_tangent: bfloat16 [14336, 6144], P('ffn', 'hid'), may hold values from -0.046875 to 0.046875
- precision: float32 [6144], P('hid'), may hold values from 1 to 10
Outputs:
- gate_product: bfloat16 [6144, 14336], P('hid', 'ffn')
- up_product: bfloat16 [6144, 14336], P('hid', 'ffn')
- down_product: bfloat16 [14336, 6144], P('ffn', 'hid')
The draws below stay inside these ranges and needn't reach their ends.
All inputs are finite; a program needn't handle non-finite values.
Results may differ from the reference program's by a relative error of at most 0.03.
Values may be sent and summed in bfloat16 or wider, within the bound.
No kernel may reach another device: no remote copies, remote signals or barrier semaphores. Data moves between devices by JAX's collectives and lax.ppermute only.
A program may use at most 128 MiB of HBM per device.

```python
import math
import jax
import jax.numpy as jnp

D = 6144
FF = 14336
TOK = 512
TOKENS = 1024
N_DP = 2


def with_spikes(drawn, rng, source, target, shards_of, factor):
    owner, partner = [(jnp.arange(drawn.shape[position]) // (drawn.shape[position] // shards_of)).reshape([-1 if axis == position else 1 for axis in range(drawn.ndim)]) for position in (source, target)]
    chosen = jax.random.permutation(rng, shards_of)[partner]
    strong = (owner == chosen) | (owner == (partner + shards_of // 2) % shards_of)
    return jnp.where(strong, factor * drawn, drawn)


def steps_of(rng, dims, pieces, low, high):
    factor_of = 1.0
    for dim, blocks in pieces:
        heights = jax.random.uniform(jax.random.fold_in(jax.random.fold_in(rng, 6), dim), (blocks,), jnp.float32, low / len(pieces), high / len(pieces))
        factor_of = factor_of * jnp.repeat(jnp.exp(heights), dims[dim] // blocks).reshape((-1,) + (1,) * (len(dims) - 1 - dim))
    return factor_of


def gaussian(rng, dims, width, reach, shards=(), held_as=jnp.bfloat16):
    values = jax.random.normal(rng, dims, jnp.float32) * width
    if len(shards) > 0:
        values = steps_of(rng, dims, shards, -0.22, 0.18) * values
    return jnp.clip(values, min=-reach, max=reach).astype(held_as)


def bell_draw_with(rng, dims, scale, bound, cuts, heavy, dtype=jnp.bfloat16):
    result = scale * jax.random.normal(rng, dims, jnp.float32)
    if cuts:
        result = result * steps_of(rng, dims, cuts, -0.22, 0.18)
    return jnp.clip(with_spikes(result, jax.random.fold_in(rng, 3), *heavy), -bound, bound).astype(dtype)


def setup_inputs(seed: int = 0) -> dict:
    keys = jax.random.split(jax.random.key(seed), 9)
    return {
        "tokens": bell_draw_with(keys[0], (TOKENS, D), 1.0, 6.0, ((0, 2), (1, 16)), (1, 0, 16, 2.0)),
        "gate_weight": gaussian(keys[1], (D, FF), D ** -0.5, 0.078125, ((0, 16), (1, 8))),
        "up_weight": gaussian(keys[2], (D, FF), D ** -0.5, 0.078125, ((0, 16), (1, 8))),
        "down_weight": gaussian(keys[3], (FF, D), FF ** -0.5, 0.046875, ((0, 8), (1, 16))),
        "gate_tangent": gaussian(keys[4], (D, FF), D ** -0.5, 0.078125, ((0, 16), (1, 8))),
        "up_tangent": gaussian(keys[5], (D, FF), D ** -0.5, 0.078125, ((0, 16), (1, 8))),
        "down_tangent": gaussian(keys[6], (FF, D), FF ** -0.5, 0.046875, ((0, 8), (1, 16))),
        "precision": jnp.clip(jnp.exp(math.log(10.0) - 2.3025851 * jax.random.uniform(keys[7], (D,), jnp.float32) ** steps_of(keys[7], (D,), ((0, 16),), -0.2, 0.2)), 1.0, 10.0),
    }


def reference(tokens, gate_weight, up_weight, down_weight, gate_tangent, up_tangent, down_tangent, precision):
    gate = jnp.dot(tokens, gate_weight, preferred_element_type=jnp.float32)
    up = jnp.dot(tokens, up_weight, preferred_element_type=jnp.float32)
    gate_dir = jnp.dot(tokens, gate_tangent, preferred_element_type=jnp.float32)
    up_dir = jnp.dot(tokens, up_tangent, preferred_element_type=jnp.float32)
    sigmoid_gate = jax.nn.sigmoid(gate)
    active = gate * sigmoid_gate
    slope = sigmoid_gate * (1.0 + gate * (1.0 - sigmoid_gate))
    hidden = (active * up).astype(jnp.bfloat16)
    hidden_dir = (slope * up * gate_dir + active * up_dir).astype(jnp.bfloat16)
    out_dir = jnp.dot(hidden_dir, down_weight, preferred_element_type=jnp.float32)
    out_dir = out_dir + jnp.dot(hidden, down_tangent, preferred_element_type=jnp.float32)
    scale = 1.0 / math.sqrt(TOKENS)
    cot = (precision[None, :] * out_dir * scale).astype(jnp.bfloat16)
    back = jnp.dot(cot, down_weight.T, preferred_element_type=jnp.float32)
    gate_adjoint = (back * slope * up).astype(jnp.bfloat16)
    up_adjoint = (back * active).astype(jnp.bfloat16)
    gate_total = jnp.zeros(gate_weight.shape, jnp.float32)
    up_total = jnp.zeros(up_weight.shape, jnp.float32)
    down_total = jnp.zeros(down_weight.shape, jnp.float32)
    for replica in range(N_DP):
        first = replica * TOK
        rows_tok = tokens[first:first + TOK]
        gate_part = jnp.dot(rows_tok.T, gate_adjoint[first:first + TOK], preferred_element_type=jnp.float32)
        up_part = jnp.dot(rows_tok.T, up_adjoint[first:first + TOK], preferred_element_type=jnp.float32)
        down_part = jnp.dot(hidden[first:first + TOK].T, cot[first:first + TOK], preferred_element_type=jnp.float32)
        gate_total = gate_total + gate_part.astype(jnp.bfloat16).astype(jnp.float32)
        up_total = up_total + up_part.astype(jnp.bfloat16).astype(jnp.float32)
        down_total = down_total + down_part.astype(jnp.bfloat16).astype(jnp.float32)
    return (gate_total.astype(jnp.bfloat16), up_total.astype(jnp.bfloat16), down_total.astype(jnp.bfloat16))
```

```python
import math

import jax
import jax.numpy as jnp
from jax import lax
from jax.sharding import Mesh, PartitionSpec as P

BF16 = jnp.bfloat16
F32 = jnp.float32
Y = ("yh", "yl")


def contract(left, right, left_dim, right_dim):
    return lax.dot_general(
        left, right, (((left_dim,), (right_dim,)), ((), ())), preferred_element_type=F32
    )


def shift(value, axis, step):
    size = lax.axis_size(axis)
    return lax.ppermute(value, axis, [(i, (i + step) % size) for i in range(size)])


def ordered(first, low, high, axis):
    return jnp.concatenate(
        [jnp.where(first, low, high), jnp.where(first, high, low)], axis=axis
    )


def ring_sum(parts, half):
    up = shift(parts(4)[:half].astype(BF16), "z", 1)
    down = shift(parts(4)[half:].astype(BF16), "z", -1)
    term = parts(3)
    up_now = jnp.concatenate([term[:half] + up.astype(F32), term[half:]], axis=0)
    term = parts(5)
    down_now = jnp.concatenate([term[:half], term[half:] + down.astype(F32)], axis=0)
    for step in (2, 1, 0):
        up = shift(up_now.astype(BF16), "z", 1).astype(F32)
        down = shift(down_now.astype(BF16), "z", -1).astype(F32)
        if step:
            up_now = parts(step) + up
            down_now = parts(8 - step) + down
    return parts(0) + up + down


def ring_gather(block, half):
    got = [block] + [None] * 7
    up, down = block, block
    for step in (1, 2, 3):
        up = shift(up, "z", 1)
        down = shift(down, "z", -1)
        got[8 - step], got[step] = up, down
    got[4] = jnp.concatenate([shift(up[:half], "z", 1), shift(down[half:], "z", -1)], axis=0)
    return got


def direct_sum(value, axis, place):
    def block(step):
        return lax.dynamic_index_in_dim(value, (place + step) % 4, 0, keepdims=False)

    got = [shift(block(step).astype(BF16), axis, step) for step in (1, 3, 2)]
    return block(0).astype(F32) + sum(part.astype(F32) for part in got)


def direct_gather(block, axis, place):
    got = [block, shift(block, axis, 3), shift(block, axis, 2), shift(block, axis, 1)]
    twice = jnp.stack(got + got[:3])
    return lax.dynamic_slice_in_dim(twice, (4 - place) % 4, 4, 0)


def on_device(
    tokens, gate_weight, up_weight, down_weight, gate_tangent, up_tangent, down_tangent, precision
):
    n_tok, width = tokens.shape
    hidden_units = gate_weight.shape[1]
    quarter = hidden_units // 4
    yh, yl, z, x, core = (lax.axis_index(name) for name in ("yh", "yl", "z", "x", "c"))
    y = 2 * yh + yl
    low = yl == 0
    scale = 1.0 / math.sqrt(2 * n_tok)

    piece = lax.dynamic_slice_in_dim(tokens, core * (n_tok // 2), n_tok // 2, 0)
    got = jnp.stack([shift(piece, Y, 1), shift(piece, Y, 2), shift(piece, Y, 3)])
    swapped = shift(got, "c", 1)
    got = ordered(core == 0, got, swapped, 1)
    below, across, above = got[0], got[1], got[2]
    near = jnp.where(low, above, below)
    far = jnp.where(low, below, above)
    top = jnp.concatenate(
        [jnp.where(yh == 0, tokens, across), jnp.where(yh == 0, near, far)], axis=1
    )
    bottom = jnp.concatenate(
        [jnp.where(yh == 0, across, tokens), jnp.where(yh == 0, far, near)], axis=1
    )
    rows = n_tok // 8
    blocks = jnp.concatenate(
        [top.reshape(8, rows, 2 * width), bottom.reshape(8, rows, 2 * width)], axis=1
    )
    blocks = lax.dynamic_slice_in_dim(jnp.concatenate([blocks, blocks[:7]]), z, 8, 0)

    half_width = width // 2

    def columns(first, second, place, start, count):
        at = (place % 4) * quarter
        return jnp.concatenate(
            [
                lax.dynamic_slice(matrix, (start, at), (count, quarter))
                for matrix in (first, second)
            ],
            axis=1,
        )

    def wide(first, second):
        own = columns(first, second, y, 0, width)
        late = shift(columns(first, second, y + 1, half_width, half_width), Y, 1)
        early = shift(columns(first, second, y + 3, 0, half_width), Y, 3)
        return jnp.concatenate([own, early, late], axis=0)

    def tall(matrix):
        def rows_of(place, start, count):
            return lax.dynamic_slice_in_dim(matrix, (place % 4) * quarter + start, count, 0)

        own = rows_of(y, 0, quarter)
        late = shift(rows_of(y + 1, quarter // 2, quarter // 2), Y, 1)
        early = shift(rows_of(y + 3, 0, quarter // 2), Y, 3)
        return ordered(low, own, jnp.concatenate([early, late], axis=0), 1)

    base = wide(gate_weight, up_weight)
    turn = wide(gate_tangent, up_tangent)
    down = tall(down_weight)
    both_down = jnp.concatenate([tall(down_tangent), down], axis=0)
    all_precision = ordered(low, precision, shift(precision, Y, 1), 0)

    values = ring_sum(lambda r: contract(base, blocks[r], 0, 1), quarter)
    turns = ring_sum(lambda r: contract(turn, blocks[r], 0, 1), quarter)
    gate, up = values[:quarter], values[quarter:]
    gate_dir, up_dir = turns[:quarter], turns[quarter:]
    sigmoid_gate = jax.nn.sigmoid(gate)
    active = gate * sigmoid_gate
    slope = sigmoid_gate * (1.0 + gate * (1.0 - sigmoid_gate))
    hidden = (active * up).astype(BF16)
    hidden_dir = (slope * up * gate_dir + active * up_dir).astype(BF16)
    coefs = jnp.concatenate([slope * up, active], axis=0).astype(BF16)

    gathered = ring_gather(jnp.concatenate([hidden, hidden_dir], axis=0), quarter)
    out = jnp.stack([contract(part, both_down, 0, 0).astype(BF16) for part in gathered])
    coefs, out = lax.optimization_barrier((coefs, out))
    all_coefs = ring_gather(coefs, quarter)

    out = out.reshape(2, 4 * 2 * rows, 2 * width)
    keep = lax.dynamic_index_in_dim(out, core, 0, keepdims=False)
    give = lax.dynamic_index_in_dim(out, 1 - core, 0, keepdims=False)
    out = (keep.astype(F32) + shift(give, "c", 1).astype(F32)).astype(BF16)
    out = out.reshape(2, 4, rows, 2 * width)
    first = direct_sum(out[0], "x", x).astype(BF16).reshape(4, rows // 4, 2 * width)
    second = direct_sum(out[1], Y, y).astype(BF16).reshape(4, rows // 4, 2 * width)
    first = direct_sum(first, Y, y)
    second = direct_sum(second, "x", x)
    first, second = (
        (all_precision[None, :] * part * scale).astype(BF16) for part in (first, second)
    )
    first = direct_gather(first, Y, y).reshape(rows, 2 * width)
    second = direct_gather(second, "x", x).reshape(rows, 2 * width)
    first = direct_gather(first, "x", x).reshape(4 * rows, 2 * width)
    second = direct_gather(second, Y, y).reshape(4 * rows, 2 * width)
    cot = jnp.concatenate([first, second], axis=0)
    cot = ordered(core == 0, cot, shift(cot, "c", 1), 0)
    cot_blocks = cot.reshape(8, 2 * rows, 2 * width)

    back = ring_sum(lambda r: contract(down, cot_blocks[r], 1, 1), quarter // 2)
    all_back = ring_gather(back.astype(BF16), quarter // 2)
    adjoint = jnp.concatenate(
        [
            (jnp.concatenate([part, part], axis=0).astype(F32) * coef.astype(F32)).astype(BF16)
            for part, coef in zip(all_back, all_coefs)
        ],
        axis=1,
    )
    all_hidden = jnp.concatenate([part[:quarter] for part in gathered], axis=1)
    down_part = contract(all_hidden, cot, 1, 0).astype(BF16)
    product = contract(blocks.reshape(2 * n_tok, 2 * width), adjoint, 0, 1).astype(BF16)

    def spread(own, other):
        pieces = [own, shift(other, Y, 3), shift(own, Y, 2), shift(other, Y, 1)]
        pieces = [jnp.where(low, pieces[i], pieces[(i + 3) % 4]) for i in range(4)]
        return [jnp.where(yh == 0, pieces[i], pieces[(i + 2) % 4]) for i in range(4)]

    left, right = down_part[:, :width], down_part[:, width:]
    down_pieces = spread(jnp.where(low, left, right), jnp.where(low, right, left))
    pieces = spread(product[:width], product[width:])
    return (
        jnp.concatenate([part[:, :quarter] for part in pieces], axis=1),
        jnp.concatenate([part[:, quarter:] for part in pieces], axis=1),
        jnp.concatenate(down_pieces, axis=0),
    )


def solution(mesh):
    fine = Mesh(mesh.devices.reshape(2, 8, 2, 4, 2), ("yh", "z", "yl", "x", "c"))
    hid, ffn = ("z", "yl"), ("x", "c")
    placed = (
        P("yh", hid),
        P(hid, ffn),
        P(hid, ffn),
        P(ffn, hid),
        P(hid, ffn),
        P(hid, ffn),
        P(ffn, hid),
        P(hid),
    )
    return jax.shard_map(
        on_device,
        mesh=fine,
        in_specs=placed,
        out_specs=(P(hid, ffn), P(hid, ffn), P(ffn, hid)),
        check_vma=False,
    )
```

```python
import math

import jax
import jax.numpy as jnp
from jax import lax
from jax.sharding import Mesh, PartitionSpec as P

BF16 = jnp.bfloat16
F32 = jnp.float32
Y = ("yh", "yl")
XY = ("x", "yh", "yl")
LANES = 128
EVEN = [(i, i ^ 1) for i in range(8)]
ODD = [(i, (i + 1 if i % 2 else i - 1) % 8) for i in range(8)]


def contract(left, right, left_dim, right_dim):
    return lax.dot_general(
        left, right, (((left_dim,), (right_dim,)), ((), ())), preferred_element_type=F32
    )


def over_even(value):
    return lax.ppermute(value, "z", EVEN)


def over_odd(value):
    return lax.ppermute(value, "z", ODD)


def swap_y(value, flip):
    return lax.ppermute(value, Y, [(i, i ^ flip) for i in range(4)])


def swap_core(value):
    return lax.ppermute(value, "c", [(0, 1), (1, 0)])


def ordered(first, low, high, axis):
    return jnp.concatenate(
        [jnp.where(first, low, high), jnp.where(first, high, low)], axis=axis
    )


def turned(tile):
    half = tile.shape[-1] // 2
    return jnp.concatenate([tile[..., half:], tile[..., :half]], axis=-1)


def halves(left, right):
    lane = lax.broadcasted_iota(jnp.int32, left.shape, left.ndim - 1)
    return jnp.where(lane < left.shape[-1] // 2, left, right)


def ring_sums(chains):
    state = []
    for parts in chains:
        far = parts(4)
        state.append((over_even(far[0]), over_odd(far[1])))
    for step in (3, 2, 1):
        after = []
        for parts, (from_even, from_odd) in zip(chains, state):
            by_even, by_odd = parts(step), parts(8 - step)
            if step == 3:
                by_even = jnp.stack(
                    [by_even[0], (by_even[1].astype(F32) + from_odd.astype(F32)).astype(BF16)]
                )
                by_odd = jnp.stack(
                    [(by_odd[0].astype(F32) + from_even.astype(F32)).astype(BF16), by_odd[1]]
                )
            else:
                by_even = (by_even.astype(F32) + from_odd.astype(F32)).astype(BF16)
                by_odd = (by_odd.astype(F32) + from_even.astype(F32)).astype(BF16)
            after.append((over_even(by_even), over_odd(by_odd)))
        state = after
    return [
        parts(0).astype(F32) + from_even.astype(F32) + from_odd.astype(F32)
        for parts, (from_even, from_odd) in zip(chains, state)
    ]


def ring_gathers(blocks):
    got = [[block] + [None] * 7 for block in blocks]
    for step in (1, 2, 3):
        for chain in got:
            by_even = chain[0] if step == 1 else chain[9 - step]
            by_odd = chain[step - 1]
            chain[step], chain[8 - step] = over_even(by_even), over_odd(by_odd)
    for chain in got:
        half = chain[0].shape[0] // 2
        chain[4] = jnp.concatenate([over_even(chain[5][:half]), over_odd(chain[3][half:])], axis=0)
    return got


def on_device(
    tokens, gate_weight, up_weight, down_weight, gate_tangent, up_tangent, down_tangent, precision
):
    n_tok, width = tokens.shape
    pair = gate_weight.shape[1] // 2
    quarter = pair // 2
    main = quarter - LANES // 2
    rows = n_tok // 8
    yh, yl, z, x, core = (lax.axis_index(name) for name in ("yh", "yl", "z", "x", "c"))
    y = 2 * yh + yl
    low = yl == 0
    scale = 1.0 / math.sqrt(2 * n_tok)

    def along(place):
        return (z + jnp.where(z % 2 == 0, place, 8 - place)) % 8

    def parity(tile):
        return jnp.where(low, tile, turned(tile))

    def apart(value):
        tile = parity(value[..., main : main + LANES])
        return (
            jnp.concatenate([value[..., :main], tile], axis=-1),
            jnp.concatenate([value[..., main + LANES :], turned(tile)], axis=-1),
        )

    def middle_of(first, second):
        return halves(first[..., main:], turned(second[..., main:]))

    edge, lanes = width // 2, 2 * quarter

    def columns(first, second, flip, rows):
        lower, even = (yh == 0) ^ (flip > 1), low ^ (flip % 2 == 1)
        parts, tiles = [], []
        for matrix in (first, second):
            held = jnp.where(lower, matrix[rows, :pair], matrix[rows, pair:])
            parts.append(jnp.where(even, held[:, :main], held[:, main + LANES :]))
            tiles.append(held[:, main : main + LANES])
        tiles[1] = turned(tiles[1])
        tile = jnp.where(even, halves(*tiles), halves(*tiles[::-1]))
        return jnp.concatenate([parts[0], tile, parts[1]], axis=1)

    def down_rows(matrix, flip):
        start = ((y ^ flip) // 2) * pair
        side = (y ^ flip) % 2
        return (
            lax.dynamic_slice_in_dim(matrix, start + side * (main + LANES), main, 0),
            lax.dynamic_slice_in_dim(matrix, start + main + side * (LANES // 2), LANES // 2, 0),
        )

    def packed(whole, part):
        tiles = [part[:, i : i + LANES] for i in range(0, width, LANES)]
        return jnp.concatenate([whole[:edge], whole[edge:], jnp.concatenate(tiles, axis=0)], axis=1)

    def unpacked(value):
        tiles = [value[i : i + LANES // 2, 2 * width :] for i in range(0, edge, LANES // 2)]
        return (
            jnp.concatenate([value[:, :width], value[:, width : 2 * width]], axis=0),
            jnp.concatenate(tiles, axis=1),
        )

    piece = lax.dynamic_slice_in_dim(tokens, core * (n_tok // 2), n_tok // 2, 0)
    got = jnp.stack([swap_y(piece, flip) for flip in (2, 1, 3)])
    got = ordered(core == 0, got, swap_core(got), 1)
    all_tokens = jnp.concatenate(
        [jnp.concatenate([tokens, got[0]], axis=0), jnp.concatenate([got[1], got[2]], axis=0)],
        axis=1,
    )
    every, upper, lower = slice(0, width), slice(0, edge), slice(edge, width)
    base_near = columns(gate_weight, up_weight, 0, every)
    base_far = [
        swap_y(columns(gate_weight, up_weight, flip, rows), flip)
        for flip, rows in ((1, upper), (3, lower))
    ]
    turn_near = columns(gate_tangent, up_tangent, 0, every)
    turn_far = [
        swap_y(
            jnp.concatenate(
                [columns(gate_tangent, up_tangent, flip, rows), packed(*down_rows(matrix, flip))],
                axis=0,
            ),
            flip,
        )
        for flip, rows, matrix in ((1, upper, down_tangent), (3, lower, down_weight))
    ]
    tangent_rows, weight_rows = (unpacked(part[edge:]) for part in turn_far)
    down_near = jnp.concatenate(
        [*down_rows(down_tangent, 0), *down_rows(down_weight, 0)[::-1]], axis=0
    )
    down_far = jnp.concatenate([*tangent_rows, *weight_rows[::-1]], axis=0)
    both_down = ordered(low, down_near, down_far, 1)
    down = jnp.concatenate(
        [
            both_down[main + LANES :],
            both_down[quarter : main + LANES],
            jnp.zeros((LANES // 2, 2 * width), BF16),
        ],
        axis=0,
    )

    def projections(near, far):
        part = contract(all_tokens, jnp.concatenate([near, *far], axis=0), 1, 0)
        return part.astype(BF16).reshape(2, 8, rows, 2 * quarter)

    def terms(part):
        return lambda place: lax.dynamic_index_in_dim(part, along(place), 1, keepdims=False)

    base_part = projections(base_near, base_far)
    turn_part = projections(turn_near, [part[:edge] for part in turn_far])
    turn_part, both_down, down = lax.optimization_barrier((turn_part, both_down, down))
    base, turn = ring_sums([terms(base_part), terms(turn_part)])
    gate, up = apart(base)
    gate_dir, up_dir = apart(turn)
    sigmoid_gate = jax.nn.sigmoid(gate)
    active = gate * sigmoid_gate
    slope = sigmoid_gate * (1.0 + gate * (1.0 - sigmoid_gate))
    hidden = (active * up).astype(BF16)
    hidden_dir = (slope * up * gate_dir + active * up_dir).astype(BF16)
    gate_coef, up_coef = slope * up, active
    block = jnp.concatenate(
        [hidden[..., :main], middle_of(hidden, hidden_dir), hidden_dir[..., :main]], axis=-1
    )

    def gather(block):
        chains = ring_gathers([block[0], block[1]])
        full = jnp.zeros((8, *block.shape), BF16)
        for place in range(8):
            part = jnp.stack([chain[place] for chain in chains])[None]
            full = lax.dynamic_update_slice_in_dim(full, part, along(place), 0)
        return full.reshape(2 * n_tok, block.shape[-1])

    all_blocks = gather(block)

    def replicas(value):
        return jnp.where(yh == 0, value, value[:, ::-1])

    def out_part(side):
        part = lax.dynamic_slice_in_dim(all_blocks, side * n_tok, n_tok, 0)
        return contract(part, both_down, 1, 0)

    give = out_part(1 - core).astype(BF16)
    out = out_part(core) + swap_core(give).astype(F32)
    out = replicas(out.reshape(4, 2, rows, 2 * width)).astype(BF16)
    out = jnp.stack([out[..., :width], out[..., width:]], axis=2)
    out = lax.all_to_all(out.reshape(16 * rows, width), XY, 0, 0, tiled=True)
    out = jnp.sum(out.reshape(16, rows, width).astype(F32), axis=0)
    cot = (precision[None, :] * out * scale).astype(BF16)
    cot = lax.all_to_all(jnp.tile(cot, (16, 1)), XY, 0, 0, tiled=True)
    cot = cot.reshape(4, 2, 2, rows, width)
    cot = replicas(jnp.concatenate([cot[:, :, 0], cot[:, :, 1]], axis=-1))
    cot = ordered(core == 0, cot, swap_core(cot), 0).reshape(2 * n_tok, 2 * width)

    back = contract(cot, down, 1, 1).astype(BF16)
    back = lax.all_to_all(back, "z", 0, 0, tiled=True).reshape(8, 2, rows, main + LANES)
    back = jnp.sum(back.astype(F32), axis=0)
    gate_adjoint = (back * gate_coef).astype(BF16)
    up_adjoint = (back * up_coef).astype(BF16)
    block = jnp.concatenate(
        [
            gate_adjoint[..., :main],
            parity(middle_of(gate_adjoint, up_adjoint)),
            up_adjoint[..., :main],
        ],
        axis=-1,
    )

    def spread(near, far):
        across = swap_y(near, 2)
        pieces = [near, swap_y(far, 1), across, swap_y(far, 3)]
        pieces = [jnp.where(low, pieces[i], pieces[i ^ 1]) for i in range(4)]
        return [jnp.where(yh == 0, pieces[i], pieces[i ^ 2]) for i in range(4)]

    down_part = contract(all_blocks[:, :quarter], cot, 0, 0).astype(BF16)
    left, right = down_part[:, :width], down_part[:, width:]
    down_pieces = spread(jnp.where(low, left, right), jnp.where(low, right, left))

    all_adjoints = gather(block)
    all_tokens = all_tokens.reshape(2, 8, rows, 2 * width)
    all_tokens = jnp.stack([all_tokens[0], all_tokens[1]], axis=1).reshape(2 * n_tok, 2 * width)
    all_adjoints, down_pieces, all_tokens = lax.optimization_barrier(
        (all_adjoints, down_pieces, all_tokens)
    )
    near_product = contract(all_tokens[:, :width], all_adjoints, 0, 0).astype(BF16)
    near_product, all_adjoints = lax.optimization_barrier((near_product, all_adjoints))
    far_product = contract(all_tokens[:, width:], all_adjoints, 0, 0).astype(BF16)
    pieces = spread(near_product, far_product)
    gate_out, up_out, down_out = [], [], []
    for first, second in (pieces[:2], pieces[2:]):
        first_tile, second_tile = first[:, main : main + LANES], second[:, main : main + LANES]
        gate_out += [first[:, :main], halves(first_tile, second_tile), second[:, :main]]
        up_out += [
            first[:, main + LANES :],
            turned(halves(second_tile, first_tile)),
            second[:, main + LANES :],
        ]
    for first, second in (down_pieces[:2], down_pieces[2:]):
        down_out += [first, second[main:], second[:main]]
    return (
        jnp.concatenate(gate_out, axis=1),
        jnp.concatenate(up_out, axis=1),
        jnp.concatenate(down_out, axis=0),
    )


def solution(mesh):
    fine = Mesh(mesh.devices.reshape(2, 8, 2, 4, 2), ("yh", "z", "yl", "x", "c"))
    hid, ffn = ("z", "yl"), ("x", "c")
    placed = (
        P("yh", hid),
        P(hid, ffn),
        P(hid, ffn),
        P(ffn, hid),
        P(hid, ffn),
        P(hid, ffn),
        P(ffn, hid),
        P(hid),
    )
    return jax.shard_map(
        on_device,
        mesh=fine,
        in_specs=placed,
        out_specs=(P(hid, ffn), P(hid, ffn), P(ffn, hid)),
        check_vma=False,
    )
```

```python
import math

import jax
import jax.numpy as jnp
from jax import lax
from jax.sharding import Mesh, PartitionSpec as P

BF16 = jnp.bfloat16
F32 = jnp.float32
Y = ("yh", "yl")
XY = ("x", "yh", "yl")
LANES = 128
EVEN = [(i, i ^ 1) for i in range(8)]
ODD = [(i, (i + 1 if i % 2 else i - 1) % 8) for i in range(8)]


def contract(left, right, left_dim, right_dim):
    return lax.dot_general(
        left, right, (((left_dim,), (right_dim,)), ((), ())), preferred_element_type=F32
    )


def over_even(value):
    return lax.ppermute(value, "z", EVEN)


def over_odd(value):
    return lax.ppermute(value, "z", ODD)


def swap_y(value, flip):
    return lax.ppermute(value, Y, [(i, i ^ flip) for i in range(4)])


def swap_core(value):
    return lax.ppermute(value, "c", [(0, 1), (1, 0)])


def ordered(first, low, high, axis):
    return jnp.concatenate(
        [jnp.where(first, low, high), jnp.where(first, high, low)], axis=axis
    )


def turned(tile):
    half = tile.shape[-1] // 2
    return jnp.concatenate([tile[..., half:], tile[..., :half]], axis=-1)


def halves(left, right):
    lane = lax.broadcasted_iota(jnp.int32, left.shape, left.ndim - 1)
    return jnp.where(lane < left.shape[-1] // 2, left, right)


def ring_sums(chains):
    state = []
    for parts in chains:
        far = parts(4)
        state.append((over_even(far[0]), over_odd(far[1])))
    for step in (3, 2, 1):
        after = []
        for parts, (from_even, from_odd) in zip(chains, state):
            by_even, by_odd = parts(step), parts(8 - step)
            if step == 3:
                by_even = jnp.stack(
                    [by_even[0], (by_even[1].astype(F32) + from_odd.astype(F32)).astype(BF16)]
                )
                by_odd = jnp.stack(
                    [(by_odd[0].astype(F32) + from_even.astype(F32)).astype(BF16), by_odd[1]]
                )
            else:
                by_even = (by_even.astype(F32) + from_odd.astype(F32)).astype(BF16)
                by_odd = (by_odd.astype(F32) + from_even.astype(F32)).astype(BF16)
            after.append((over_even(by_even), over_odd(by_odd)))
        state = after
    return [
        parts(0).astype(F32) + from_even.astype(F32) + from_odd.astype(F32)
        for parts, (from_even, from_odd) in zip(chains, state)
    ]


def ring_gathers(blocks):
    got = [[block] + [None] * 7 for block in blocks]
    for step in (1, 2, 3):
        for chain in got:
            by_even = chain[0] if step == 1 else chain[9 - step]
            by_odd = chain[step - 1]
            chain[step], chain[8 - step] = over_even(by_even), over_odd(by_odd)
    for chain in got:
        half = chain[0].shape[0] // 2
        chain[4] = jnp.concatenate([over_even(chain[5][:half]), over_odd(chain[3][half:])], axis=0)
    return got


def on_device(
    tokens, gate_weight, up_weight, down_weight, gate_tangent, up_tangent, down_tangent, precision
):
    n_tok, width = tokens.shape
    pair = gate_weight.shape[1] // 2
    quarter = pair // 2
    main = quarter - LANES // 2
    rows = n_tok // 8
    yh, yl, z, x, core = (lax.axis_index(name) for name in ("yh", "yl", "z", "x", "c"))
    y = 2 * yh + yl
    low = yl == 0
    scale = 1.0 / math.sqrt(2 * n_tok)

    def along(place):
        return (z + jnp.where(z % 2 == 0, place, 8 - place)) % 8

    def parity(tile):
        return jnp.where(low, tile, turned(tile))

    def apart(value):
        tile = parity(value[..., main : main + LANES])
        return (
            jnp.concatenate([value[..., :main], tile], axis=-1),
            jnp.concatenate([value[..., main + LANES :], turned(tile)], axis=-1),
        )

    def middle_of(first, second):
        return halves(first[..., main:], turned(second[..., main:]))

    edge, lanes = width // 2, 2 * quarter

    def columns(first, second, flip, rows):
        lower, even = (yh == 0) ^ (flip > 1), low ^ (flip % 2 == 1)
        parts, tiles = [], []
        for matrix in (first, second):
            held = jnp.where(lower, matrix[rows, :pair], matrix[rows, pair:])
            parts.append(jnp.where(even, held[:, :main], held[:, main + LANES :]))
            tiles.append(held[:, main : main + LANES])
        tiles[1] = turned(tiles[1])
        tile = jnp.where(even, halves(*tiles), halves(*tiles[::-1]))
        return jnp.concatenate([parts[0], tile, parts[1]], axis=1)

    def down_rows(matrix, flip):
        start = ((y ^ flip) // 2) * pair
        side = (y ^ flip) % 2
        return (
            lax.dynamic_slice_in_dim(matrix, start + side * (main + LANES), main, 0),
            lax.dynamic_slice_in_dim(matrix, start + main + side * (LANES // 2), LANES // 2, 0),
        )

    def packed(whole, part):
        tiles = [part[:, i : i + LANES] for i in range(0, width, LANES)]
        return jnp.concatenate([whole[:edge], whole[edge:], jnp.concatenate(tiles, axis=0)], axis=1)

    def unpacked(value):
        tiles = [value[i : i + LANES // 2, 2 * width :] for i in range(0, edge, LANES // 2)]
        return (
            jnp.concatenate([value[:, :width], value[:, width : 2 * width]], axis=0),
            jnp.concatenate(tiles, axis=1),
        )

    piece = lax.dynamic_slice_in_dim(tokens, core * (n_tok // 2), n_tok // 2, 0)
    got = jnp.stack([swap_y(piece, flip) for flip in (2, 1, 3)])
    got = ordered(core == 0, got, swap_core(got), 1)
    all_tokens = jnp.concatenate(
        [jnp.concatenate([tokens, got[0]], axis=0), jnp.concatenate([got[1], got[2]], axis=0)],
        axis=1,
    )
    every, upper, lower = slice(0, width), slice(0, edge), slice(edge, width)
    base_near = columns(gate_weight, up_weight, 0, every)
    base_far = [
        columns(gate_weight, up_weight, flip, rows) for flip, rows in ((1, upper), (3, lower))
    ]
    base_far, gate_tangent, up_tangent, down_tangent, down_weight = lax.optimization_barrier(
        (base_far, gate_tangent, up_tangent, down_tangent, down_weight)
    )
    base_far = [swap_y(part, flip) for part, flip in zip(base_far, (1, 3))]
    turn_near = columns(gate_tangent, up_tangent, 0, every)
    turn_far = [
        swap_y(
            jnp.concatenate(
                [columns(gate_tangent, up_tangent, flip, rows), packed(*down_rows(matrix, flip))],
                axis=0,
            ),
            flip,
        )
        for flip, rows, matrix in ((1, upper, down_tangent), (3, lower, down_weight))
    ]
    tangent_rows, weight_rows = (unpacked(part[edge:]) for part in turn_far)
    down_near = jnp.concatenate(
        [*down_rows(down_tangent, 0), *down_rows(down_weight, 0)[::-1]], axis=0
    )
    down_far = jnp.concatenate([*tangent_rows, *weight_rows[::-1]], axis=0)
    both_down = ordered(low, down_near, down_far, 1)
    down = jnp.concatenate(
        [
            both_down[main + LANES :],
            both_down[quarter : main + LANES],
            jnp.zeros((LANES // 2, 2 * width), BF16),
        ],
        axis=0,
    )

    def projections(near, far):
        part = contract(all_tokens, jnp.concatenate([near, *far], axis=0), 1, 0)
        return part.astype(BF16).reshape(2, 8, rows, 2 * quarter)

    def terms(part):
        return lambda place: lax.dynamic_index_in_dim(part, along(place), 1, keepdims=False)

    base_part = projections(base_near, base_far)
    turn_part = projections(turn_near, [part[:edge] for part in turn_far])
    base, turn = ring_sums([terms(base_part), terms(turn_part)])
    gate, up = apart(base)
    gate_dir, up_dir = apart(turn)
    sigmoid_gate = jax.nn.sigmoid(gate)
    active = gate * sigmoid_gate
    slope = sigmoid_gate * (1.0 + gate * (1.0 - sigmoid_gate))
    hidden = (active * up).astype(BF16)
    hidden_dir = (slope * up * gate_dir + active * up_dir).astype(BF16)
    gate_coef, up_coef = slope * up, active
    block = jnp.concatenate(
        [hidden[..., :main], middle_of(hidden, hidden_dir), hidden_dir[..., :main]], axis=-1
    )

    def gather(block):
        chains = ring_gathers([block[0], block[1]])
        full = jnp.zeros((8, *block.shape), BF16)
        for place in range(8):
            part = jnp.stack([chain[place] for chain in chains])[None]
            full = lax.dynamic_update_slice_in_dim(full, part, along(place), 0)
        return full.reshape(2 * n_tok, block.shape[-1])

    block, both_down, down = lax.optimization_barrier((block, both_down, down))
    all_blocks = gather(block)

    def replicas(value):
        return jnp.where(yh == 0, value, value[:, ::-1])

    def out_part(side):
        part = lax.dynamic_slice_in_dim(all_blocks, side * n_tok, n_tok, 0)
        return contract(part, both_down, 1, 0)

    give = out_part(1 - core).astype(BF16)
    out = out_part(core) + swap_core(give).astype(F32)
    out = replicas(out.reshape(4, 2, rows, 2 * width)).astype(BF16)
    out = jnp.stack([out[..., :width], out[..., width:]], axis=2)
    out = lax.all_to_all(out.reshape(16 * rows, width), XY, 0, 0, tiled=True)
    out = jnp.sum(out.reshape(16, rows, width).astype(F32), axis=0)
    cot = (precision[None, :] * out * scale).astype(BF16)
    cot = lax.all_to_all(jnp.tile(cot, (16, 1)), XY, 0, 0, tiled=True)
    cot = cot.reshape(4, 2, 2, rows, width)
    cot = replicas(jnp.concatenate([cot[:, :, 0], cot[:, :, 1]], axis=-1))
    cot = ordered(core == 0, cot, swap_core(cot), 0).reshape(2 * n_tok, 2 * width)

    back = contract(cot, down, 1, 1).astype(BF16)
    back = lax.all_to_all(back, "z", 0, 0, tiled=True).reshape(8, 2, rows, main + LANES)
    back = jnp.sum(back.astype(F32), axis=0)
    gate_adjoint = (back * gate_coef).astype(BF16)
    up_adjoint = (back * up_coef).astype(BF16)
    block = jnp.concatenate(
        [
            gate_adjoint[..., :main],
            parity(middle_of(gate_adjoint, up_adjoint)),
            up_adjoint[..., :main],
        ],
        axis=-1,
    )

    def spread(near, far):
        across = swap_y(near, 2)
        pieces = [near, swap_y(far, 1), across, swap_y(far, 3)]
        pieces = [jnp.where(low, pieces[i], pieces[i ^ 1]) for i in range(4)]
        return [jnp.where(yh == 0, pieces[i], pieces[i ^ 2]) for i in range(4)]

    down_part = contract(all_blocks[:, :quarter], cot, 0, 0).astype(BF16)
    left, right = down_part[:, :width], down_part[:, width:]
    down_pieces = spread(jnp.where(low, left, right), jnp.where(low, right, left))

    all_adjoints = gather(block)
    all_tokens = all_tokens.reshape(2, 8, rows, 2 * width)
    all_tokens = jnp.stack([all_tokens[0], all_tokens[1]], axis=1).reshape(2 * n_tok, 2 * width)
    all_adjoints, down_pieces, all_tokens = lax.optimization_barrier(
        (all_adjoints, down_pieces, all_tokens)
    )
    near_product = contract(all_tokens[:, :width], all_adjoints, 0, 0).astype(BF16)
    near_product, all_adjoints = lax.optimization_barrier((near_product, all_adjoints))
    far_product = contract(all_tokens[:, width:], all_adjoints, 0, 0).astype(BF16)
    pieces = spread(near_product, far_product)
    gate_out, up_out, down_out = [], [], []
    for first, second in (pieces[:2], pieces[2:]):
        first_tile, second_tile = first[:, main : main + LANES], second[:, main : main + LANES]
        gate_out += [first[:, :main], halves(first_tile, second_tile), second[:, :main]]
        up_out += [
            first[:, main + LANES :],
            turned(halves(second_tile, first_tile)),
            second[:, main + LANES :],
        ]
    for first, second in (down_pieces[:2], down_pieces[2:]):
        down_out += [first, second[main:], second[:main]]
    return (
        jnp.concatenate(gate_out, axis=1),
        jnp.concatenate(up_out, axis=1),
        jnp.concatenate(down_out, axis=0),
    )


def solution(mesh):
    fine = Mesh(mesh.devices.reshape(2, 8, 2, 4, 2), ("yh", "z", "yl", "x", "c"))
    hid, ffn = ("z", "yl"), ("x", "c")
    placed = (
        P("yh", hid),
        P(hid, ffn),
        P(hid, ffn),
        P(ffn, hid),
        P(hid, ffn),
        P(hid, ffn),
        P(ffn, hid),
        P(hid),
    )
    return jax.shard_map(
        on_device,
        mesh=fine,
        in_specs=placed,
        out_specs=(P(hid, ffn), P(hid, ffn), P(ffn, hid)),
        check_vma=False,
    )
```

```python
import math

import jax
import jax.numpy as jnp
from jax import lax
from jax.sharding import Mesh, PartitionSpec as P

BF16 = jnp.bfloat16
F32 = jnp.float32
Y = ("yh", "yl")
XY = ("x", "yh", "yl")
LANES = 128
EVEN = [(i, i ^ 1) for i in range(8)]
ODD = [(i, (i + 1 if i % 2 else i - 1) % 8) for i in range(8)]


def contract(left, right, left_dim, right_dim):
    return lax.dot_general(
        left, right, (((left_dim,), (right_dim,)), ((), ())), preferred_element_type=F32
    )


def over_even(value):
    return lax.ppermute(value, "z", EVEN)


def over_odd(value):
    return lax.ppermute(value, "z", ODD)


def swap_y(value, flip):
    return lax.ppermute(value, Y, [(i, i ^ flip) for i in range(4)])


def swap_core(value):
    return lax.ppermute(value, "c", [(0, 1), (1, 0)])


def ordered(first, low, high, axis):
    return jnp.concatenate(
        [jnp.where(first, low, high), jnp.where(first, high, low)], axis=axis
    )


def turned(tile):
    half = tile.shape[-1] // 2
    return jnp.concatenate([tile[..., half:], tile[..., :half]], axis=-1)


def halves(left, right):
    lane = lax.broadcasted_iota(jnp.int32, left.shape, left.ndim - 1)
    return jnp.where(lane < left.shape[-1] // 2, left, right)


def ring_sums(chains):
    state = []
    for parts in chains:
        far = parts(4)
        state.append((over_even(far[0]), over_odd(far[1])))
    for step in (3, 2, 1):
        after = []
        for parts, (from_even, from_odd) in zip(chains, state):
            by_even, by_odd = parts(step), parts(8 - step)
            if step == 3:
                by_even = jnp.stack(
                    [by_even[0], (by_even[1].astype(F32) + from_odd.astype(F32)).astype(BF16)]
                )
                by_odd = jnp.stack(
                    [(by_odd[0].astype(F32) + from_even.astype(F32)).astype(BF16), by_odd[1]]
                )
            else:
                by_even = (by_even.astype(F32) + from_odd.astype(F32)).astype(BF16)
                by_odd = (by_odd.astype(F32) + from_even.astype(F32)).astype(BF16)
            after.append((over_even(by_even), over_odd(by_odd)))
        state = after
    return [
        parts(0).astype(F32) + from_even.astype(F32) + from_odd.astype(F32)
        for parts, (from_even, from_odd) in zip(chains, state)
    ]


def ring_gathers(blocks):
    got = [[block] + [None] * 7 for block in blocks]
    for step in (1, 2, 3):
        for chain in got:
            by_even = chain[0] if step == 1 else chain[9 - step]
            by_odd = chain[step - 1]
            chain[step], chain[8 - step] = over_even(by_even), over_odd(by_odd)
    for chain in got:
        half = chain[0].shape[0] // 2
        chain[4] = jnp.concatenate([over_even(chain[5][:half]), over_odd(chain[3][half:])], axis=0)
    return got


def on_device(
    tokens, gate_weight, up_weight, down_weight, gate_tangent, up_tangent, down_tangent, precision
):
    n_tok, width = tokens.shape
    pair = gate_weight.shape[1] // 2
    quarter = pair // 2
    main = quarter - LANES // 2
    rows = n_tok // 8
    yh, yl, z, x, core = (lax.axis_index(name) for name in ("yh", "yl", "z", "x", "c"))
    y = 2 * yh + yl
    low = yl == 0
    scale = 1.0 / math.sqrt(2 * n_tok)

    def along(place):
        return (z + jnp.where(z % 2 == 0, place, 8 - place)) % 8

    def parity(tile):
        return jnp.where(low, tile, turned(tile))

    def apart(value):
        tile = parity(value[..., main : main + LANES])
        return (
            jnp.concatenate([value[..., :main], tile], axis=-1),
            jnp.concatenate([value[..., main + LANES :], turned(tile)], axis=-1),
        )

    def middle_of(first, second):
        return halves(first[..., main:], turned(second[..., main:]))

    edge, lanes = width // 2, 2 * quarter

    def columns(first, second, flip, rows):
        lower, even = (yh == 0) ^ (flip > 1), low ^ (flip % 2 == 1)
        parts, tiles = [], []
        for matrix in (first, second):
            held = jnp.where(lower, matrix[rows, :pair], matrix[rows, pair:])
            parts.append(jnp.where(even, held[:, :main], held[:, main + LANES :]))
            tiles.append(held[:, main : main + LANES])
        tiles[1] = turned(tiles[1])
        tile = jnp.where(even, halves(*tiles), halves(*tiles[::-1]))
        return jnp.concatenate([parts[0], tile, parts[1]], axis=1)

    def down_rows(matrix, flip):
        start = ((y ^ flip) // 2) * pair
        side = (y ^ flip) % 2
        return (
            lax.dynamic_slice_in_dim(matrix, start + side * (main + LANES), main, 0),
            lax.dynamic_slice_in_dim(matrix, start + main + side * (LANES // 2), LANES // 2, 0),
        )

    def packed(whole, part):
        tiles = [part[:, i : i + LANES] for i in range(0, width, LANES)]
        return jnp.concatenate([whole[:edge], whole[edge:], jnp.concatenate(tiles, axis=0)], axis=1)

    def unpacked(value):
        tiles = [value[i : i + LANES // 2, 2 * width :] for i in range(0, edge, LANES // 2)]
        return (
            jnp.concatenate([value[:, :width], value[:, width : 2 * width]], axis=0),
            jnp.concatenate(tiles, axis=1),
        )

    piece = lax.dynamic_slice_in_dim(tokens, core * (n_tok // 2), n_tok // 2, 0)
    got = jnp.stack([swap_y(piece, flip) for flip in (2, 1, 3)])
    swapped = swap_core(got)
    every, upper, lower = slice(0, width), slice(0, edge), slice(edge, width)
    base_near = columns(gate_weight, up_weight, 0, every)
    base_far = [
        columns(gate_weight, up_weight, flip, rows) for flip, rows in ((1, upper), (3, lower))
    ]
    base_far, gate_tangent, up_tangent, down_tangent, down_weight = lax.optimization_barrier(
        (base_far, gate_tangent, up_tangent, down_tangent, down_weight)
    )
    base_far, swapped = lax.optimization_barrier((base_far, swapped))
    base_far = [swap_y(part, flip) for part, flip in zip(base_far, (1, 3))]
    got = ordered(core == 0, got, swapped, 1)
    all_tokens = jnp.concatenate(
        [jnp.concatenate([tokens, got[0]], axis=0), jnp.concatenate([got[1], got[2]], axis=0)],
        axis=1,
    )
    turn_near = columns(gate_tangent, up_tangent, 0, every)
    turn_far = [
        swap_y(
            jnp.concatenate(
                [columns(gate_tangent, up_tangent, flip, rows), packed(*down_rows(matrix, flip))],
                axis=0,
            ),
            flip,
        )
        for flip, rows, matrix in ((1, upper, down_tangent), (3, lower, down_weight))
    ]
    tangent_rows, weight_rows = (unpacked(part[edge:]) for part in turn_far)
    down_near = jnp.concatenate(
        [*down_rows(down_tangent, 0), *down_rows(down_weight, 0)[::-1]], axis=0
    )
    down_far = jnp.concatenate([*tangent_rows, *weight_rows[::-1]], axis=0)
    both_down = ordered(low, down_near, down_far, 1)
    down = jnp.concatenate(
        [
            both_down[main + LANES :],
            both_down[quarter : main + LANES],
            jnp.zeros((LANES // 2, 2 * width), BF16),
        ],
        axis=0,
    )

    def projections(near, far):
        part = contract(all_tokens, jnp.concatenate([near, *far], axis=0), 1, 0)
        return part.astype(BF16).reshape(2, 8, rows, 2 * quarter)

    def terms(part):
        return lambda place: lax.dynamic_index_in_dim(part, along(place), 1, keepdims=False)

    base_part = projections(base_near, base_far)
    turn_part = projections(turn_near, [part[:edge] for part in turn_far])
    base, turn = ring_sums([terms(base_part), terms(turn_part)])
    gate, up = apart(base)
    gate_dir, up_dir = apart(turn)
    sigmoid_gate = jax.nn.sigmoid(gate)
    active = gate * sigmoid_gate
    slope = sigmoid_gate * (1.0 + gate * (1.0 - sigmoid_gate))
    hidden = (active * up).astype(BF16)
    hidden_dir = (slope * up * gate_dir + active * up_dir).astype(BF16)
    gate_coef, up_coef = slope * up, active
    block = jnp.concatenate(
        [hidden[..., :main], middle_of(hidden, hidden_dir), hidden_dir[..., :main]], axis=-1
    )

    def gather(block):
        chains = ring_gathers([block[0], block[1]])
        full = jnp.zeros((8, *block.shape), BF16)
        for place in range(8):
            part = jnp.stack([chain[place] for chain in chains])[None]
            full = lax.dynamic_update_slice_in_dim(full, part, along(place), 0)
        return full.reshape(2 * n_tok, block.shape[-1])

    block, both_down, down = lax.optimization_barrier((block, both_down, down))
    all_blocks = gather(block)

    def replicas(value):
        return jnp.where(yh == 0, value, value[:, ::-1])

    def out_part(side):
        part = lax.dynamic_slice_in_dim(all_blocks, side * n_tok, n_tok, 0)
        return contract(part, both_down, 1, 0)

    give = out_part(1 - core).astype(BF16)
    out = out_part(core) + swap_core(give).astype(F32)
    out = replicas(out.reshape(4, 2, rows, 2 * width)).astype(BF16)
    out = jnp.stack([out[..., :width], out[..., width:]], axis=2)
    out = lax.all_to_all(out.reshape(16 * rows, width), XY, 0, 0, tiled=True)
    out = jnp.sum(out.reshape(16, rows, width).astype(F32), axis=0)
    cot = (precision[None, :] * out * scale).astype(BF16)
    cot = lax.all_to_all(jnp.tile(cot, (16, 1)), XY, 0, 0, tiled=True)
    cot = cot.reshape(4, 2, 2, rows, width)
    cot = replicas(jnp.concatenate([cot[:, :, 0], cot[:, :, 1]], axis=-1))
    cot = ordered(core == 0, cot, swap_core(cot), 0).reshape(2 * n_tok, 2 * width)

    back = contract(cot, down, 1, 1).astype(BF16)
    back = lax.all_to_all(back, "z", 0, 0, tiled=True).reshape(8, 2, rows, main + LANES)
    back = jnp.sum(back.astype(F32), axis=0)
    gate_adjoint = (back * gate_coef).astype(BF16)
    up_adjoint = (back * up_coef).astype(BF16)
    block = jnp.concatenate(
        [
            gate_adjoint[..., :main],
            parity(middle_of(gate_adjoint, up_adjoint)),
            up_adjoint[..., :main],
        ],
        axis=-1,
    )

    def spread(near, far):
        across = swap_y(near, 2)
        pieces = [near, swap_y(far, 1), across, swap_y(far, 3)]
        pieces = [jnp.where(low, pieces[i], pieces[i ^ 1]) for i in range(4)]
        return [jnp.where(yh == 0, pieces[i], pieces[i ^ 2]) for i in range(4)]

    down_part = contract(all_blocks[:, :quarter], cot, 0, 0).astype(BF16)
    left, right = down_part[:, :width], down_part[:, width:]
    down_pieces = spread(jnp.where(low, left, right), jnp.where(low, right, left))

    all_adjoints = gather(block)
    all_tokens = all_tokens.reshape(2, 8, rows, 2 * width)
    all_tokens = jnp.stack([all_tokens[0], all_tokens[1]], axis=1).reshape(2 * n_tok, 2 * width)
    all_adjoints, down_pieces, all_tokens = lax.optimization_barrier(
        (all_adjoints, down_pieces, all_tokens)
    )
    near_product = contract(all_tokens[:, :width], all_adjoints, 0, 0).astype(BF16)
    near_product, all_adjoints = lax.optimization_barrier((near_product, all_adjoints))
    far_product = contract(all_tokens[:, width:], all_adjoints, 0, 0).astype(BF16)
    pieces = spread(near_product, far_product)
    gate_out, up_out, down_out = [], [], []
    for first, second in (pieces[:2], pieces[2:]):
        first_tile, second_tile = first[:, main : main + LANES], second[:, main : main + LANES]
        gate_out += [first[:, :main], halves(first_tile, second_tile), second[:, :main]]
        up_out += [
            first[:, main + LANES :],
            turned(halves(second_tile, first_tile)),
            second[:, main + LANES :],
        ]
    for first, second in (down_pieces[:2], down_pieces[2:]):
        down_out += [first, second[main:], second[:main]]
    return (
        jnp.concatenate(gate_out, axis=1),
        jnp.concatenate(up_out, axis=1),
        jnp.concatenate(down_out, axis=0),
    )


def solution(mesh):
    fine = Mesh(mesh.devices.reshape(2, 8, 2, 4, 2), ("yh", "z", "yl", "x", "c"))
    hid, ffn = ("z", "yl"), ("x", "c")
    placed = (
        P("yh", hid),
        P(hid, ffn),
        P(hid, ffn),
        P(ffn, hid),
        P(hid, ffn),
        P(hid, ffn),
        P(ffn, hid),
        P(hid),
    )
    return jax.shard_map(
        on_device,
        mesh=fine,
        in_specs=placed,
        out_specs=(P(hid, ffn), P(hid, ffn), P(ffn, hid)),
        check_vma=False,
    )
```

```python
import math

import jax
import jax.numpy as jnp
from jax import lax
from jax.sharding import Mesh, PartitionSpec as P

BF16 = jnp.bfloat16
F32 = jnp.float32
Y = ("yh", "yl")
XY = ("x", "yh", "yl")
LANES = 128
EVEN = [(i, i ^ 1) for i in range(8)]
ODD = [(i, (i + 1 if i % 2 else i - 1) % 8) for i in range(8)]


def contract(left, right, left_dim, right_dim):
    return lax.dot_general(
        left, right, (((left_dim,), (right_dim,)), ((), ())), preferred_element_type=F32
    )


def over_even(value):
    return lax.ppermute(value, "z", EVEN)


def over_odd(value):
    return lax.ppermute(value, "z", ODD)


def swap_y(value, flip):
    return lax.ppermute(value, Y, [(i, i ^ flip) for i in range(4)])


def swap_core(value):
    return lax.ppermute(value, "c", [(0, 1), (1, 0)])


def ordered(first, low, high, axis):
    return jnp.concatenate(
        [jnp.where(first, low, high), jnp.where(first, high, low)], axis=axis
    )


def turned(tile):
    half = tile.shape[-1] // 2
    return jnp.concatenate([tile[..., half:], tile[..., :half]], axis=-1)


def halves(left, right):
    lane = lax.broadcasted_iota(jnp.int32, left.shape, left.ndim - 1)
    return jnp.where(lane < left.shape[-1] // 2, left, right)


def ring_sums(chains):
    state = []
    for parts in chains:
        far = parts(4)
        state.append((over_even(far[0]), over_odd(far[1])))
    for step in (3, 2, 1):
        after = []
        for parts, (from_even, from_odd) in zip(chains, state):
            by_even, by_odd = parts(step), parts(8 - step)
            if step == 3:
                by_even = jnp.stack(
                    [by_even[0], (by_even[1].astype(F32) + from_odd.astype(F32)).astype(BF16)]
                )
                by_odd = jnp.stack(
                    [(by_odd[0].astype(F32) + from_even.astype(F32)).astype(BF16), by_odd[1]]
                )
            else:
                by_even = (by_even.astype(F32) + from_odd.astype(F32)).astype(BF16)
                by_odd = (by_odd.astype(F32) + from_even.astype(F32)).astype(BF16)
            after.append((over_even(by_even), over_odd(by_odd)))
        state = after
    return [
        parts(0).astype(F32) + from_even.astype(F32) + from_odd.astype(F32)
        for parts, (from_even, from_odd) in zip(chains, state)
    ]


def ring_gathers(blocks):
    got = [[block] + [None] * 7 for block in blocks]
    for step in (1, 2, 3):
        for chain in got:
            by_even = chain[0] if step == 1 else chain[9 - step]
            by_odd = chain[step - 1]
            chain[step], chain[8 - step] = over_even(by_even), over_odd(by_odd)
    for chain in got:
        half = chain[0].shape[0] // 2
        chain[4] = jnp.concatenate([over_even(chain[5][:half]), over_odd(chain[3][half:])], axis=0)
    return got


def on_device(
    tokens, gate_weight, up_weight, down_weight, gate_tangent, up_tangent, down_tangent, precision
):
    n_tok, width = tokens.shape
    pair = gate_weight.shape[1] // 2
    quarter = pair // 2
    main = quarter - LANES // 2
    rows = n_tok // 8
    yh, yl, z, x, core = (lax.axis_index(name) for name in ("yh", "yl", "z", "x", "c"))
    y = 2 * yh + yl
    low = yl == 0
    scale = 1.0 / math.sqrt(2 * n_tok)

    def along(place):
        return (z + jnp.where(z % 2 == 0, place, 8 - place)) % 8

    def parity(tile):
        return jnp.where(low, tile, turned(tile))

    def apart(value):
        tile = parity(value[..., main : main + LANES])
        return (
            jnp.concatenate([value[..., :main], tile], axis=-1),
            jnp.concatenate([value[..., main + LANES :], turned(tile)], axis=-1),
        )

    def middle_of(first, second):
        return halves(first[..., main:], turned(second[..., main:]))

    edge, lanes = width // 2, 2 * quarter

    def columns(first, second, flip, rows):
        lower, even = (yh == 0) ^ (flip > 1), low ^ (flip % 2 == 1)
        parts, tiles = [], []
        for matrix in (first, second):
            held = jnp.where(lower, matrix[rows, :pair], matrix[rows, pair:])
            parts.append(jnp.where(even, held[:, :main], held[:, main + LANES :]))
            tiles.append(held[:, main : main + LANES])
        tiles[1] = turned(tiles[1])
        tile = jnp.where(even, halves(*tiles), halves(*tiles[::-1]))
        return jnp.concatenate([parts[0], tile, parts[1]], axis=1)

    def down_rows(matrix, flip):
        start = ((y ^ flip) // 2) * pair
        side = (y ^ flip) % 2
        return (
            lax.dynamic_slice_in_dim(matrix, start + side * (main + LANES), main, 0),
            lax.dynamic_slice_in_dim(matrix, start + main + side * (LANES // 2), LANES // 2, 0),
        )

    def packed(whole, part):
        tiles = [part[:, i : i + LANES] for i in range(0, width, LANES)]
        return jnp.concatenate([whole[:edge], whole[edge:], jnp.concatenate(tiles, axis=0)], axis=1)

    def unpacked(value):
        tiles = [value[i : i + LANES // 2, 2 * width :] for i in range(0, edge, LANES // 2)]
        return (
            jnp.concatenate([value[:, :width], value[:, width : 2 * width]], axis=0),
            jnp.concatenate(tiles, axis=1),
        )

    piece = lax.dynamic_slice_in_dim(tokens, core * (n_tok // 2), n_tok // 2, 0)
    got = jnp.stack([swap_y(piece, flip) for flip in (2, 1, 3)])
    got = ordered(core == 0, got, swap_core(got), 1)
    all_tokens = jnp.concatenate(
        [jnp.concatenate([tokens, got[0]], axis=0), jnp.concatenate([got[1], got[2]], axis=0)],
        axis=1,
    )
    every, upper, lower = slice(0, width), slice(0, edge), slice(edge, width)
    base_near = columns(gate_weight, up_weight, 0, every)
    base_far = [
        columns(gate_weight, up_weight, flip, rows) for flip, rows in ((1, upper), (3, lower))
    ]
    base_far, gate_tangent, up_tangent, down_tangent, down_weight = lax.optimization_barrier(
        (base_far, gate_tangent, up_tangent, down_tangent, down_weight)
    )
    base_far = [swap_y(part, flip) for part, flip in zip(base_far, (1, 3))]
    turn_near = columns(gate_tangent, up_tangent, 0, every)
    turn_far = [
        swap_y(
            jnp.concatenate(
                [columns(gate_tangent, up_tangent, flip, rows), packed(*down_rows(matrix, flip))],
                axis=0,
            ),
            flip,
        )
        for flip, rows, matrix in ((1, upper, down_tangent), (3, lower, down_weight))
    ]
    tangent_rows, weight_rows = (unpacked(part[edge:]) for part in turn_far)
    down_near = jnp.concatenate(
        [*down_rows(down_tangent, 0), *down_rows(down_weight, 0)[::-1]], axis=0
    )
    down_far = jnp.concatenate([*tangent_rows, *weight_rows[::-1]], axis=0)
    both_down = ordered(low, down_near, down_far, 1)
    down = jnp.concatenate(
        [
            both_down[main + LANES :],
            both_down[quarter : main + LANES],
            jnp.zeros((LANES // 2, 2 * width), BF16),
        ],
        axis=0,
    )

    def projections(near, far):
        part = contract(all_tokens[:, :width], near, 1, 0)
        part = part + contract(all_tokens[:, width:], jnp.concatenate(far, axis=0), 1, 0)
        return part.astype(BF16).reshape(2, 8, rows, 2 * quarter)

    def terms(part):
        return lambda place: lax.dynamic_index_in_dim(part, along(place), 1, keepdims=False)

    base_part = projections(base_near, base_far)
    turn_part = projections(turn_near, [part[:edge] for part in turn_far])
    base, turn = ring_sums([terms(base_part), terms(turn_part)])
    gate, up = apart(base)
    gate_dir, up_dir = apart(turn)
    sigmoid_gate = jax.nn.sigmoid(gate)
    active = gate * sigmoid_gate
    slope = sigmoid_gate * (1.0 + gate * (1.0 - sigmoid_gate))
    hidden = (active * up).astype(BF16)
    hidden_dir = (slope * up * gate_dir + active * up_dir).astype(BF16)
    gate_coef, up_coef = slope * up, active
    block = jnp.concatenate(
        [hidden[..., :main], middle_of(hidden, hidden_dir), hidden_dir[..., :main]], axis=-1
    )

    def gather(block):
        chains = ring_gathers([block[0], block[1]])
        full = jnp.zeros((8, *block.shape), BF16)
        for place in range(8):
            part = jnp.stack([chain[place] for chain in chains])[None]
            full = lax.dynamic_update_slice_in_dim(full, part, along(place), 0)
        return full.reshape(2 * n_tok, block.shape[-1])

    block, both_down, down = lax.optimization_barrier((block, both_down, down))
    all_blocks = gather(block)

    def replicas(value):
        return jnp.where(yh == 0, value, value[:, ::-1])

    def out_part(side):
        part = lax.dynamic_slice_in_dim(all_blocks, side * n_tok, n_tok, 0)
        return contract(part, both_down, 1, 0)

    give = out_part(1 - core).astype(BF16)
    out = out_part(core) + swap_core(give).astype(F32)
    out = replicas(out.reshape(4, 2, rows, 2 * width)).astype(BF16)
    out = jnp.stack([out[..., :width], out[..., width:]], axis=2)
    out = lax.all_to_all(out.reshape(16 * rows, width), XY, 0, 0, tiled=True)
    out = jnp.sum(out.reshape(16, rows, width).astype(F32), axis=0)
    cot = (precision[None, :] * out * scale).astype(BF16)
    cot = lax.all_to_all(jnp.tile(cot, (16, 1)), XY, 0, 0, tiled=True)
    cot = cot.reshape(4, 2, 2, rows, width)
    cot = replicas(jnp.concatenate([cot[:, :, 0], cot[:, :, 1]], axis=-1))
    cot = ordered(core == 0, cot, swap_core(cot), 0).reshape(2 * n_tok, 2 * width)

    back = contract(cot, down, 1, 1).astype(BF16)
    back = lax.all_to_all(back, "z", 0, 0, tiled=True).reshape(8, 2, rows, main + LANES)
    back = jnp.sum(back.astype(F32), axis=0)
    gate_adjoint = (back * gate_coef).astype(BF16)
    up_adjoint = (back * up_coef).astype(BF16)
    block = jnp.concatenate(
        [
            gate_adjoint[..., :main],
            parity(middle_of(gate_adjoint, up_adjoint)),
            up_adjoint[..., :main],
        ],
        axis=-1,
    )

    def spread(near, far):
        across = swap_y(near, 2)
        pieces = [near, swap_y(far, 1), across, swap_y(far, 3)]
        pieces = [jnp.where(low, pieces[i], pieces[i ^ 1]) for i in range(4)]
        return [jnp.where(yh == 0, pieces[i], pieces[i ^ 2]) for i in range(4)]

    down_part = contract(all_blocks[:, :quarter], cot, 0, 0).astype(BF16)
    left, right = down_part[:, :width], down_part[:, width:]
    down_pieces = spread(jnp.where(low, left, right), jnp.where(low, right, left))

    all_adjoints = gather(block)
    all_tokens = all_tokens.reshape(2, 8, rows, 2 * width)
    all_tokens = jnp.stack([all_tokens[0], all_tokens[1]], axis=1).reshape(2 * n_tok, 2 * width)
    all_adjoints, down_pieces, all_tokens = lax.optimization_barrier(
        (all_adjoints, down_pieces, all_tokens)
    )
    near_product = contract(all_tokens[:, :width], all_adjoints, 0, 0).astype(BF16)
    near_product, all_adjoints = lax.optimization_barrier((near_product, all_adjoints))
    far_product = contract(all_tokens[:, width:], all_adjoints, 0, 0).astype(BF16)
    pieces = spread(near_product, far_product)
    gate_out, up_out, down_out = [], [], []
    for first, second in (pieces[:2], pieces[2:]):
        first_tile, second_tile = first[:, main : main + LANES], second[:, main : main + LANES]
        gate_out += [first[:, :main], halves(first_tile, second_tile), second[:, :main]]
        up_out += [
            first[:, main + LANES :],
            turned(halves(second_tile, first_tile)),
            second[:, main + LANES :],
        ]
    for first, second in (down_pieces[:2], down_pieces[2:]):
        down_out += [first, second[main:], second[:main]]
    return (
        jnp.concatenate(gate_out, axis=1),
        jnp.concatenate(up_out, axis=1),
        jnp.concatenate(down_out, axis=0),
    )


def solution(mesh):
    fine = Mesh(mesh.devices.reshape(2, 8, 2, 4, 2), ("yh", "z", "yl", "x", "c"))
    hid, ffn = ("z", "yl"), ("x", "c")
    placed = (
        P("yh", hid),
        P(hid, ffn),
        P(hid, ffn),
        P(ffn, hid),
        P(hid, ffn),
        P(hid, ffn),
        P(ffn, hid),
        P(hid),
    )
    return jax.shard_map(
        on_device,
        mesh=fine,
        in_specs=placed,
        out_specs=(P(hid, ffn), P(hid, ffn), P(ffn, hid)),
        check_vma=False,
    )
```
